32 devices in a mesh: seq: 16 (over z, y, core), head: 2 (over x).
Axes of the slice: x: 2, y: 2, z: 4, core: 2. Of those that a mesh axis runs over, the one named last changes fastest.
Arguments:
- mixer_query: bfloat16 [4096, 4096], P('seq', 'head'), may hold values from -13 to 13
- mixer_key: bfloat16 [4096, 4096], P('seq', 'head'), may hold values from -6 to 6
- mixer_value: bfloat16 [4096, 4096], P('seq', 'head'), may hold values from -6 to 6
- shift_taps: float32 [8, 4096], P(None, 'head'), may hold values from -2 to 2
- conv_kernel: float32 [4096, 4096], P(('head', 'seq')), may hold values from -2 to 2
- heads_query: bfloat16 [4096, 4096], P('seq', 'head'), may hold values from -6 to 6
- heads_key: bfloat16 [4096, 4096], P('seq', 'head'), may hold values from -6 to 6
- heads_value: bfloat16 [4096, 4096], P('seq', 'head'), may hold values from -6 to 6
- beta_attention: float32 [4096], P('head'), may hold values from 0.5 to 2
- beta_mixer: float32 [4096], P('head'), may hold values from 0.5 to 2
Outputs:
- block_output: bfloat16 [4096, 4096], P('seq', 'head')
The draws below stay inside these ranges and needn't reach their ends.
All inputs are finite; a program needn't handle non-finite values.
Results may differ from the reference program's by a relative error of at most 0.0053.
Values may be sent and summed in bfloat16 or wider, within the bound.
A program may use at most 128 MiB of HBM per device.

```python
import math
import jax
import jax.numpy as jnp
from jax import lax

D = 4096
HD = 128
TAPS = 8
SPAN = 3
TOK_DEV = 256
LENGTH = 4096


def clipped(key, shape, bound):
    return jnp.clip(jax.random.normal(key, shape, jnp.float32), -bound, bound)


def attention_pair(key):
    base_query = clipped(jax.random.fold_in(key, 11), (LENGTH, D), 4.0)
    base_key = clipped(jax.random.fold_in(key, 12), (LENGTH, D), 4.0)
    return (base_query, base_key)


def draw_heads_query(key, part):
    return attention_pair(key)[0].astype(jnp.bfloat16)


def draw_heads_key(key, part):
    return attention_pair(key)[1].astype(jnp.bfloat16)


def draw_mixer_query(key, part):
    values = clipped(key, (LENGTH, D), 4.0)
    column = jnp.arange(D, dtype=jnp.float32)[None, :] / D
    return (values * 0.5 * jnp.exp(column * math.log(3.0))).astype(jnp.bfloat16)


def draw_conv_kernel(key, part):
    pick = jax.random.uniform(jax.random.fold_in(key, 1), (D, 1), jnp.float32)
    slow = jnp.exp(jax.random.uniform(jax.random.fold_in(key, 2), (D, 1), jnp.float32, math.log(0.25 / LENGTH), math.log(2.0 / LENGTH)))
    fast = jnp.exp(jax.random.uniform(jax.random.fold_in(key, 3), (D, 1), jnp.float32, math.log(1.0 / 50.0), math.log(1.0 / 25.0)))
    noise = clipped(jax.random.fold_in(key, 4), (D, LENGTH), 6.0)
    places = jnp.arange(LENGTH, dtype=jnp.float32)[None, :]
    rate = jnp.where(pick < 0.5, slow, fast)
    envelope = jnp.sqrt(2.0 * rate) * jnp.exp(-rate * places)
    return envelope * noise


def shard_levels(own_key, extent, cuts, low, top_value):
    level, own = 1.0, jax.random.fold_in(own_key, 6)
    for position, shards_of in cuts:
        heights = jnp.exp(jax.random.uniform(jax.random.fold_in(own, position), (shards_of,), jnp.float32, low / len(cuts), top_value / len(cuts)))
        level = level * jnp.repeat(heights, extent[position] // shards_of).reshape([-1 if axis == position else 1 for axis in range(len(extent))])
    return level


def gaussian(key, dims, spread, limit, pieces=(), held_as=jnp.bfloat16):
    entries = spread * jax.random.normal(key, dims, jnp.float32)
    if pieces:
        entries = entries * shard_levels(key, dims, pieces, -0.22, 0.18)
    return jnp.clip(entries, -limit, limit).astype(held_as)


def setup_inputs(seed: int = 0) -> dict:
    key_list = jax.random.split(jax.random.key(seed), 11)
    mixer_query = draw_mixer_query(jax.random.fold_in(key_list[10], 71), 0)
    mixer_key = gaussian(key_list[1], (LENGTH, D), 1.0, 6.0, ((0, 16), (1, 2)))
    mixer_value = gaussian(key_list[2], (LENGTH, D), 1.0, 6.0, ((0, 16), (1, 2)))
    shift_taps = gaussian(key_list[3], (TAPS, D), TAPS ** -0.5, 2.0, ((1, 2),), jnp.float32)
    conv_kernel = draw_conv_kernel(jax.random.fold_in(key_list[10], 71), 0)
    heads_query = draw_heads_query(jax.random.fold_in(key_list[10], 71), 0)
    heads_key = draw_heads_key(jax.random.fold_in(key_list[10], 71), 0)
    heads_value = gaussian(key_list[7], (LENGTH, D), 1.0, 6.0, ((0, 16), (1, 2)))
    beta_attention = jnp.clip(jnp.exp(math.log(2.0) - 1.3862944 * jax.random.uniform(key_list[8], (D,), jnp.float32) ** shard_levels(key_list[8], (D,), ((0, 2),), -0.2, 0.2)), 0.5, 2.0)
    beta_mixer = jnp.clip(jnp.exp(math.log(2.0) - 1.3862944 * jax.random.uniform(key_list[9], (D,), jnp.float32) ** shard_levels(key_list[9], (D,), ((0, 2),), -0.2, 0.2)), 0.5, 2.0)
    return dict(mixer_query=mixer_query, mixer_key=mixer_key, mixer_value=mixer_value, shift_taps=shift_taps, conv_kernel=conv_kernel, heads_query=heads_query, heads_key=heads_key, heads_value=heads_value, beta_attention=beta_attention, beta_mixer=beta_mixer)


def shift_conv(keys, taps):
    count = keys.shape[0]
    width = taps.shape[0]
    source = jnp.concatenate([jnp.zeros((width - 1, keys.shape[1]), jnp.float32), keys.astype(jnp.float32)], 0)
    total = jnp.zeros((count, keys.shape[1]), jnp.float32)
    for offset in range(width):
        total = total + taps[offset][None, :] * source[width - 1 - offset:width - 1 - offset + count]
    return total

def long_conv(signal, kernel):
    length = signal.shape[1]
    period = 2 * length
    group = 64
    number = signal.shape[0] // group

    def one(pair):
        part_signal, part_kernel = pair
        spectrum = jnp.fft.rfft(part_signal, n=period, axis=1) * jnp.fft.rfft(part_kernel, n=period, axis=1)
        return jnp.fft.irfft(spectrum, n=period, axis=1)[:, :length]
    result = lax.map(one, (signal.reshape(number, group, length), kernel.reshape(number, group, length)))
    return result.reshape(signal.shape[0], length)

def attention(query, keys, values):
    length, width = query.shape
    heads = width // HD
    scale = 1.0 / math.sqrt(HD)
    front = SPAN * TOK_DEV
    pad_keys = jnp.concatenate([jnp.zeros((front, width), keys.dtype), keys], 0)
    pad_values = jnp.concatenate([jnp.zeros((front, width), values.dtype), values], 0)

    def block(index):
        start = (index * TOK_DEV).astype(jnp.int32)
        rows_query = lax.dynamic_slice_in_dim(query, start, TOK_DEV, 0).astype(jnp.float32).reshape(TOK_DEV, heads, HD)
        rows_key = lax.dynamic_slice_in_dim(pad_keys, start, front + TOK_DEV, 0).astype(jnp.float32).reshape(front + TOK_DEV, heads, HD)
        rows_value = lax.dynamic_slice_in_dim(pad_values, start, front + TOK_DEV, 0).astype(jnp.float32).reshape(front + TOK_DEV, heads, HD)
        scores = jnp.einsum('qhd,khd->hqk', rows_query, rows_key, precision=lax.Precision.HIGHEST) * scale
        query_pos = start + jnp.arange(TOK_DEV, dtype=jnp.int32)
        key_pos = start - front + jnp.arange(front + TOK_DEV, dtype=jnp.int32)
        visible = (key_pos[None, :] <= query_pos[:, None]) & (key_pos[None, :] >= 0)
        scores = jnp.where(visible[None], scores, -1e+30)
        top = lax.optimization_barrier(jnp.max(scores, axis=2, keepdims=True))
        probs = jnp.exp(scores - top)
        weights = lax.optimization_barrier(probs.astype(jnp.bfloat16)).astype(jnp.float32)
        numer = jnp.einsum('hqk,khd->qhd', weights, rows_value, precision=lax.Precision.HIGHEST)
        total = lax.optimization_barrier(jnp.sum(probs, axis=2))
        return (numer / jnp.transpose(total)[:, :, None]).reshape(TOK_DEV, width)
    blocks = jnp.arange(length // TOK_DEV, dtype=jnp.int32)
    return lax.map(block, blocks).reshape(length, width)

def reference(mixer_query, mixer_key, mixer_value, shift_taps, conv_kernel, heads_query, heads_key, heads_value, beta_attention, beta_mixer):
    shifted = shift_conv(mixer_key, shift_taps)
    ssm_input = (shifted * mixer_value.astype(jnp.float32)).astype(jnp.bfloat16)
    signal = jnp.transpose(ssm_input).astype(jnp.float32)
    ssm_output = jnp.transpose(long_conv(signal, conv_kernel)).astype(jnp.bfloat16)
    mixer_branch = mixer_query.astype(jnp.float32) * ssm_output.astype(jnp.float32)
    attention_branch = attention(heads_query, heads_key, heads_value)
    attention_square = lax.optimization_barrier(jnp.sum(attention_branch * attention_branch, axis=1, keepdims=True)) / D
    mixer_square = lax.optimization_barrier(jnp.sum(mixer_branch * mixer_branch, axis=1, keepdims=True)) / D
    joined = beta_attention[None, :] * attention_branch * lax.rsqrt(attention_square + 1e-05) + beta_mixer[None, :] * mixer_branch * lax.rsqrt(mixer_square + 1e-05)
    return (joined * 0.5).astype(jnp.bfloat16)
```

```python
import functools
import math

import jax
import jax.numpy as jnp
import ml_dtypes
import numpy as np
from jax import lax
from jax.experimental import pallas as pl
from jax.experimental.pallas import tpu as pltpu
from jax.sharding import PartitionSpec as P

D = 4096
HD = 128
TAPS = 8
SPAN = 3
EDGE = 16
EPS = 1e-05
F32 = jnp.float32
BF16 = jnp.bfloat16
VMEM = pl.BlockSpec(memory_space=pltpu.VMEM)


def params(mib, **more):
    return pltpu.CompilerParams(vmem_limit_bytes=mib * 2**20, **more)


def moved(block, distance):
    count = lax.axis_size("seq")
    return lax.ppermute(block, "seq", [(i, i + distance) for i in range(count - distance)])


def shift_kernel(key_ref, before_ref, value_ref, taps_ref, out_ref, ext_ref):
    count, width = key_ref.shape
    ext_ref[0:EDGE, :] = before_ref[...].astype(F32)
    ext_ref[EDGE:, :] = key_ref[...].astype(F32)
    total = taps_ref[0:1, :] * ext_ref[EDGE : EDGE + count, :]
    for j in range(1, TAPS):
        total = total + taps_ref[j : j + 1, :] * ext_ref[EDGE - j : EDGE - j + count, :]
    product = (total * value_ref[...].astype(F32)).astype(BF16)
    for g in range(width // 128):
        out_ref[g] = product[:, g * 128 : (g + 1) * 128]


def shift_filter(key, before, value, taps):
    count, width = key.shape
    step = min(width, 512)
    return pl.pallas_call(
        shift_kernel,
        grid=(width // step,),
        in_specs=[
            pl.BlockSpec((count, step), lambda g: (0, g)),
            pl.BlockSpec((EDGE, step), lambda g: (0, g)),
            pl.BlockSpec((count, step), lambda g: (0, g)),
            pl.BlockSpec((TAPS, step), lambda g: (0, g)),
        ],
        out_specs=pl.BlockSpec((step // 128, count, 128), lambda g: (g, 0, 0)),
        out_shape=jax.ShapeDtypeStruct((width // 128, count, 128), BF16),
        scratch_shapes=[pltpu.VMEM((count + EDGE, step), F32)],
        compiler_params=params(32),
        name="shift",
    )(key, before, value, taps)


def fft(values, sign):
    n = len(values)
    if n == 1:
        return values
    even = fft(values[0::2], sign)
    odd = fft(values[1::2], sign)
    low, high = [], []
    for k in range(n // 2):
        er, ei = even[k]
        orr, oi = odd[k]
        if k == 0:
            tr, ti = orr, oi
        elif 4 * k == n:
            tr, ti = (-oi, orr) if sign > 0 else (oi, -orr)
        else:
            c = math.cos(2 * math.pi * k / n)
            s = sign * math.sin(2 * math.pi * k / n)
            if 8 * k == n:
                tr, ti = ((orr - oi) * c, (orr + oi) * c) if sign > 0 else ((orr + oi) * c, (oi - orr) * c)
            elif 8 * k == 3 * n:
                h = -c
                tr, ti = ((-orr - oi) * h, (orr - oi) * h) if sign > 0 else ((oi - orr) * h, (-orr - oi) * h)
            else:
                tr, ti = orr * c - oi * s, orr * s + oi * c
        low.append((er + tr, ei + ti))
        high.append((er - tr, ei - ti))
    return low + high


def plan(length):
    return 32 if length <= 8192 else 64


def split(table):
    high = table.astype(ml_dtypes.bfloat16)
    low = (table - high.astype(np.float64)).astype(ml_dtypes.bfloat16)
    return high, low


def tables(length):
    outer = plan(length)
    inner = length // outer
    period = 2 * length
    b = np.arange(inner)
    angle = 2 * np.pi / inner * (np.outer(b, b) % inner)
    c, s = np.cos(angle), np.sin(angle)
    forward = np.block([[c, s], [-s, c]])
    twist = 2 * np.pi / period * np.outer(b, 2 * np.arange(outer) + 0.5)
    return (
        split(forward),
        split(forward.T),
        np.cos(twist).astype(np.float32),
        np.sin(twist).astype(np.float32),
    )


def dot(a, b):
    return jnp.dot(a, b, preferred_element_type=F32)


def dot3(gh_ref, gl_ref, z):
    zh = z.astype(BF16)
    zl = (z - zh.astype(F32)).astype(BF16)
    gh = gh_ref[...]
    return dot(gh, zh) + dot(gh, zl) + dot(gl_ref[...], zh)


def outer_forward(xf_ref, z_ref, c_ref, s_ref, outer):
    inner = c_ref.shape[0]

    def body(i, carry):
        r = pl.multiple_of(i * 8, 8)
        values = []
        for a in range(outer):
            x = xf_ref[pl.ds(pl.multiple_of(a * inner + r, 8), 8), :]
            w = math.pi * a / (2 * outer)
            values.append((x * math.cos(w), x * (-math.sin(w))))
        values = fft(values, -1)
        c, s = c_ref[pl.ds(r, 8), :], s_ref[pl.ds(r, 8), :]
        for k in range(outer):
            zr, zi = values[k]
            ck, sk = c[:, k : k + 1], s[:, k : k + 1]
            z_ref[k, pl.ds(r, 8), :] = zr * ck + zi * sk
            z_ref[k, pl.ds(pl.multiple_of(inner + r, 8), 8), :] = zi * ck - zr * sk
        return carry

    lax.fori_loop(0, inner // 8, body, 0)


def outer_inverse(z_ref, xf_ref, c_ref, s_ref, outer):
    inner = c_ref.shape[0]

    def body(i, carry):
        r = pl.multiple_of(i * 8, 8)
        c, s = c_ref[pl.ds(r, 8), :], s_ref[pl.ds(r, 8), :]
        values = []
        for k in range(outer):
            zr = z_ref[k, pl.ds(r, 8), :]
            zi = z_ref[k, pl.ds(pl.multiple_of(inner + r, 8), 8), :]
            ck, sk = c[:, k : k + 1], s[:, k : k + 1]
            values.append((zr * ck - zi * sk, zi * ck + zr * sk))
        values = fft(values, 1)
        for a in range(outer):
            w = math.pi * a / (2 * outer)
            scale = 1.0 / (outer * inner)
            y = values[a][0] * (scale * math.cos(w)) - values[a][1] * (scale * math.sin(w))
            xf_ref[pl.ds(pl.multiple_of(a * inner + r, 8), 8), :] = y
        return carry

    lax.fori_loop(0, inner // 8, body, 0)


def kernel_spectrum_kernel(outer, ker_ref, gh_ref, gl_ref, c_ref, s_ref, out_ref, xf_ref, z_ref):
    inner = c_ref.shape[0]
    for a in range(outer):
        xf_ref[a * inner : (a + 1) * inner, :] = ker_ref[:, a * inner : (a + 1) * inner].T
    outer_forward(xf_ref, z_ref, c_ref, s_ref, outer)

    def body(j, carry):
        z = jnp.concatenate([z_ref[2 * j], z_ref[2 * j + 1]], axis=1)
        h = dot3(gh_ref, gl_ref, z)
        number = h.shape[1] // 2
        out_ref[2 * j] = h[:, :number]
        out_ref[2 * j + 1] = h[:, number:]
        return carry

    lax.fori_loop(0, outer // 2, body, 0)


def conv_kernel_body(outer, sig_ref, spec_ref, gh_ref, gl_ref, ih_ref, il_ref, c_ref, s_ref, out_ref, xf_ref, z_ref):
    inner = c_ref.shape[0]
    xf_ref[...] = sig_ref[...].astype(F32)
    outer_forward(xf_ref, z_ref, c_ref, s_ref, outer)

    def body(j, carry):
        z = jnp.concatenate([z_ref[2 * j], z_ref[2 * j + 1]], axis=1)
        h = jnp.concatenate([spec_ref[2 * j], spec_ref[2 * j + 1]], axis=1)
        f = dot3(gh_ref, gl_ref, z)
        fr, fi = f[:inner], f[inner:]
        hr, hi = h[:inner], h[inner:]
        p = jnp.concatenate([fr * hr - fi * hi, fr * hi + fi * hr], axis=0)
        w = dot3(ih_ref, il_ref, p)
        number = w.shape[1] // 2
        z_ref[2 * j] = w[:, :number]
        z_ref[2 * j + 1] = w[:, number:]
        return carry

    lax.fori_loop(0, outer // 2, body, 0)
    outer_inverse(z_ref, xf_ref, c_ref, s_ref, outer)
    out_ref[...] = xf_ref[...].astype(BF16)


def kernel_spectrum(kernel):
    number, length = kernel.shape
    outer = plan(length)
    inner = length // outer
    (gh, gl), _, c, s = tables(length)
    return pl.pallas_call(
        functools.partial(kernel_spectrum_kernel, outer),
        in_specs=[VMEM] * 5,
        out_specs=VMEM,
        out_shape=jax.ShapeDtypeStruct((outer, 2 * inner, number), F32),
        scratch_shapes=[
            pltpu.VMEM((length, number), F32),
            pltpu.VMEM((outer, 2 * inner, number), F32),
        ],
        compiler_params=params(60),
        cost_estimate=pl.CostEstimate(flops=6 * 10**9, bytes_accessed=7 * 2**20, transcendentals=0),
        name="kernel_spectrum",
    )(kernel, gh, gl, c, s)


def long_conv(signal, spectrum):
    length, number = signal.shape
    outer = plan(length)
    inner = length // outer
    (gh, gl), (ih, il), c, s = tables(length)
    return pl.pallas_call(
        functools.partial(conv_kernel_body, outer),
        in_specs=[VMEM] * 8,
        out_specs=VMEM,
        out_shape=jax.ShapeDtypeStruct((length, number), BF16),
        scratch_shapes=[
            pltpu.VMEM((length, number), F32),
            pltpu.VMEM((outer, 2 * inner, number), F32),
        ],
        compiler_params=params(60),
        cost_estimate=pl.CostEstimate(flops=12 * 10**9, bytes_accessed=7 * 2**20, transcendentals=0),
        name="long_conv",
    )(signal, spectrum, gh, gl, ih, il, c, s)


def row_sums(square):
    ones = jnp.ones((8, square.shape[1]), F32)
    return lax.dot_general(
        ones, square, (((1,), (1,)), ((), ())), precision=lax.Precision.HIGHEST, preferred_element_type=F32
    )


def attention_kernel(*refs):
    query_ref = refs[0]
    keys = refs[1 : 2 + SPAN]
    values = refs[2 + SPAN : 3 + 2 * SPAN]
    out_ref, sum_ref, acc_ref = refs[3 + 2 * SPAN :]
    count, width = query_ref.shape
    step = pl.program_id(0)
    me = lax.axis_index("seq")

    @pl.when(step == 0)
    def _():
        acc_ref[...] = jnp.zeros_like(acc_ref)

    row = lax.broadcasted_iota(jnp.int32, (count, count), 0)
    col = lax.broadcasted_iota(jnp.int32, (count, count), 1)
    causal = col <= row
    scale = math.log2(math.e) / math.sqrt(HD)
    for h in range(width // HD):
        lanes = slice(h * HD, (h + 1) * HD)
        q = query_ref[:, lanes]
        scores = []
        for j in range(SPAN + 1):
            s = lax.dot_general(q, keys[j][:, lanes], (((1,), (1,)), ((), ())), preferred_element_type=F32)
            if j == 0:
                s = jnp.where(causal, s, -1e30)
            else:
                s = jnp.where(me >= j, s, -1e30)
            scores.append(s)
        peak = functools.reduce(jnp.maximum, scores)
        top = jnp.max(peak, axis=1, keepdims=True)
        numer = jnp.zeros((count, HD), F32)
        total = jnp.zeros((count, count), F32)
        for j in range(SPAN + 1):
            p = jnp.exp2((scores[j] - top) * scale)
            total = total + p
            numer = numer + dot(p.astype(BF16), values[j][:, lanes])
        o = numer / jnp.sum(total, axis=1, keepdims=True)
        out_ref[:, lanes] = o
        acc_ref[...] += o * o

    @pl.when(step == pl.num_programs(0) - 1)
    def _():
        sum_ref[...] = row_sums(acc_ref[...])


def attention(query, keys, values):
    count, width = query.shape
    step = min(width, 256)
    block = pl.BlockSpec((count, step), lambda g: (0, g))
    return pl.pallas_call(
        attention_kernel,
        grid=(width // step,),
        in_specs=[block] * (3 + 2 * SPAN),
        out_specs=[block, pl.BlockSpec((8, count), lambda g: (0, 0))],
        out_shape=[
            jax.ShapeDtypeStruct((count, width), F32),
            jax.ShapeDtypeStruct((8, count), F32),
        ],
        scratch_shapes=[pltpu.VMEM((count, HD), F32)],
        compiler_params=params(40),
        cost_estimate=pl.CostEstimate(flops=5 * 10**9, bytes_accessed=11 * 2**20, transcendentals=4 * 10**6),
        name="attention",
    )(query, *keys, *values)


def mixer_sums_kernel(query_ref, filtered_ref, sum_ref):
    groups, count, lanes = filtered_ref.shape
    acc = jnp.zeros((count, lanes), F32)
    for g in range(groups):
        m = query_ref[:, g * lanes : (g + 1) * lanes].astype(F32) * filtered_ref[g].astype(F32)
        acc = acc + m * m
    sum_ref[...] = row_sums(acc)


def mixer_sums(query, filtered):
    return pl.pallas_call(
        mixer_sums_kernel,
        in_specs=[VMEM] * 2,
        out_specs=VMEM,
        out_shape=jax.ShapeDtypeStruct((8, query.shape[0]), F32),
        compiler_params=params(32),
        name="mixer_sums",
    )(query, filtered)


def join_kernel(attn_ref, query_ref, filtered_ref, asum_ref, msum_ref, beta_a_ref, beta_m_ref, out_ref):
    lanes = filtered_ref.shape[2]
    a_scale = (0.5 * lax.rsqrt(asum_ref[...] / D + EPS)).T[:, 0:1]
    m_scale = (0.5 * lax.rsqrt(msum_ref[...] / D + EPS)).T[:, 0:1]
    for g in range(filtered_ref.shape[0]):
        at = slice(g * lanes, (g + 1) * lanes)
        m = query_ref[:, at].astype(F32) * filtered_ref[g].astype(F32)
        y = beta_a_ref[:, at] * (attn_ref[:, at] * a_scale) + beta_m_ref[:, at] * (m * m_scale)
        out_ref[:, at] = y.astype(BF16)


def join(attn, query, filtered, asum, msum, beta_a, beta_m):
    count, width = query.shape
    step = min(width, 512)
    block = pl.BlockSpec((count, step), lambda g: (0, g))
    sums = pl.BlockSpec((8, count), lambda g: (0, 0))
    beta = pl.BlockSpec((1, step), lambda g: (0, g))
    return pl.pallas_call(
        join_kernel,
        grid=(width // step,),
        in_specs=[block, block, pl.BlockSpec((step // 128, count, 128), lambda g: (g, 0, 0)), sums, sums, beta, beta],
        out_specs=block,
        out_shape=jax.ShapeDtypeStruct((count, width), BF16),
        compiler_params=params(32),
        name="join",
    )(attn, query, filtered, asum, msum, beta_a[None, :], beta_m[None, :])


def on_device(
    mixer_query,
    mixer_key,
    mixer_value,
    shift_taps,
    conv_kernel,
    heads_query,
    heads_key,
    heads_value,
    beta_attention,
    beta_mixer,
):
    count, width = mixer_key.shape
    devices = lax.axis_size("seq")
    number, length = conv_kernel.shape
    before = moved(mixer_key[count - EDGE :], 1)
    ssm_input = shift_filter(mixer_key, before, mixer_value, shift_taps)
    if number != 128:
        ssm_input = jnp.transpose(ssm_input, (1, 0, 2)).reshape(count, devices, number)
        ssm_input = jnp.transpose(ssm_input, (1, 0, 2))
    signal = lax.all_to_all(ssm_input, "seq", split_axis=0, concat_axis=0, tiled=True)
    spectrum = kernel_spectrum(conv_kernel)
    keys = [heads_key] + [moved(heads_key, j) for j in range(1, SPAN + 1)]
    values = [heads_value] + [moved(heads_value, j) for j in range(1, SPAN + 1)]
    filtered = long_conv(signal.reshape(length, number), spectrum)
    filtered = filtered.reshape(devices, count, number)
    returned = lax.all_to_all(filtered, "seq", split_axis=0, concat_axis=0, tiled=True)
    if number != 128:
        returned = jnp.transpose(returned, (1, 0, 2)).reshape(count, width // 128, 128)
        returned = jnp.transpose(returned, (1, 0, 2))
    attn, asum = attention(heads_query, keys, values)
    msum = mixer_sums(mixer_query, returned)
    asum = lax.psum(asum, "head")
    msum = lax.psum(msum, "head")
    return join(attn, mixer_query, returned, asum, msum, beta_attention, beta_mixer)


def solution(mesh):
    return jax.shard_map(
        on_device,
        mesh=mesh,
        in_specs=(
            P("seq", "head"),
            P("seq", "head"),
            P("seq", "head"),
            P(None, "head"),
            P(("head", "seq"), None),
            P("seq", "head"),
            P("seq", "head"),
            P("seq", "head"),
            P("head"),
            P("head"),
        ),
        out_specs=P("seq", "head"),
        check_vma=False,
    )
```

```python
import functools
import math

import jax
import jax.numpy as jnp
import ml_dtypes
import numpy as np
from jax import lax
from jax.experimental import pallas as pl
from jax.experimental.pallas import tpu as pltpu
from jax.sharding import PartitionSpec as P

D = 4096
HD = 128
TAPS = 8
SPAN = 3
EDGE = 16
EPS = 1e-05
F32 = jnp.float32
BF16 = jnp.bfloat16
VMEM = pl.BlockSpec(memory_space=pltpu.VMEM)


def params(mib, **more):
    return pltpu.CompilerParams(vmem_limit_bytes=mib * 2**20, **more)


def moved(block, distance):
    count = lax.axis_size("seq")
    return lax.ppermute(block, "seq", [(i, i + distance) for i in range(count - distance)])


def routed(block, pairs):
    count = lax.axis_size("seq")
    return lax.ppermute(block, "seq", [(i, j) for i, j in pairs if 0 <= j < count])


def earlier(block):
    ids = range(lax.axis_size("seq"))
    two = routed(block, [(i, i + 2) for i in ids])
    cross = routed(block, [(i, i + 1 + 2 * (i % 2)) for i in ids])
    swapped = routed(two, [(i, i + 1 - 2 * (i % 2)) for i in ids])
    return [two, swapped, cross]


def shift_kernel(key_ref, before_ref, value_ref, taps_ref, out_ref, ext_ref):
    count, width = key_ref.shape
    ext_ref[0:EDGE, :] = before_ref[...].astype(F32)
    ext_ref[EDGE:, :] = key_ref[...].astype(F32)
    total = taps_ref[0:1, :] * ext_ref[EDGE : EDGE + count, :]
    for j in range(1, TAPS):
        total = total + taps_ref[j : j + 1, :] * ext_ref[EDGE - j : EDGE - j + count, :]
    product = (total * value_ref[...].astype(F32)).astype(BF16)
    for g in range(width // 128):
        out_ref[g] = product[:, g * 128 : (g + 1) * 128]


def shift_filter(key, before, value, taps):
    count, width = key.shape
    step = min(width, 512)
    return pl.pallas_call(
        shift_kernel,
        grid=(width // step,),
        in_specs=[
            pl.BlockSpec((count, step), lambda g: (0, g)),
            pl.BlockSpec((EDGE, step), lambda g: (0, g)),
            pl.BlockSpec((count, step), lambda g: (0, g)),
            pl.BlockSpec((TAPS, step), lambda g: (0, g)),
        ],
        out_specs=pl.BlockSpec((step // 128, count, 128), lambda g: (g, 0, 0)),
        out_shape=jax.ShapeDtypeStruct((width // 128, count, 128), BF16),
        scratch_shapes=[pltpu.VMEM((count + EDGE, step), F32)],
        compiler_params=params(60),
        name="shift",
    )(key, before, value, taps)


def fft(values, sign):
    n = len(values)
    if n == 1:
        return values
    even = fft(values[0::2], sign)
    odd = fft(values[1::2], sign)
    low, high = [], []
    for k in range(n // 2):
        er, ei = even[k]
        orr, oi = odd[k]
        if k == 0:
            tr, ti = orr, oi
        elif 4 * k == n:
            tr, ti = (-oi, orr) if sign > 0 else (oi, -orr)
        else:
            c = math.cos(2 * math.pi * k / n)
            s = sign * math.sin(2 * math.pi * k / n)
            if 8 * k == n:
                tr, ti = ((orr - oi) * c, (orr + oi) * c) if sign > 0 else ((orr + oi) * c, (oi - orr) * c)
            elif 8 * k == 3 * n:
                h = -c
                tr, ti = ((-orr - oi) * h, (orr - oi) * h) if sign > 0 else ((oi - orr) * h, (-orr - oi) * h)
            else:
                tr, ti = orr * c - oi * s, orr * s + oi * c
        low.append((er + tr, ei + ti))
        high.append((er - tr, ei - ti))
    return low + high


def plan(length):
    return 32 if length <= 8192 else 64


def split(table):
    high = table.astype(ml_dtypes.bfloat16)
    low = (table - high.astype(np.float64)).astype(ml_dtypes.bfloat16)
    return high, low


def tables(length):
    outer = plan(length)
    inner = length // outer
    period = 2 * length
    b = np.arange(inner)
    angle = 2 * np.pi / inner * (np.outer(b, b) % inner)
    c, s = np.cos(angle), np.sin(angle)
    forward = np.block([[c, s], [-s, c]])
    twist = 2 * np.pi / period * np.outer(b, 2 * np.arange(outer) + 0.5)
    return (
        split(forward),
        split(forward.T),
        np.cos(twist).astype(np.float32),
        np.sin(twist).astype(np.float32),
    )


def dot(a, b):
    return jnp.dot(a, b, preferred_element_type=F32)


def dot3(gh_ref, gl_ref, z):
    zh = z.astype(BF16)
    zl = (z - zh.astype(F32)).astype(BF16)
    gh = gh_ref[...]
    return dot(gh, zh) + dot(gh, zl) + dot(gl_ref[...], zh)


def outer_forward(xf_ref, z_ref, c_ref, s_ref, outer):
    inner = c_ref.shape[0]

    def body(i, carry):
        r = pl.multiple_of(i * 8, 8)
        values = []
        for a in range(outer):
            x = xf_ref[pl.ds(pl.multiple_of(a * inner + r, 8), 8), :]
            w = math.pi * a / (2 * outer)
            values.append((x * math.cos(w), x * (-math.sin(w))))
        values = fft(values, -1)
        c, s = c_ref[pl.ds(r, 8), :], s_ref[pl.ds(r, 8), :]
        for k in range(outer):
            zr, zi = values[k]
            ck, sk = c[:, k : k + 1], s[:, k : k + 1]
            z_ref[k, pl.ds(r, 8), :] = zr * ck + zi * sk
            z_ref[k, pl.ds(pl.multiple_of(inner + r, 8), 8), :] = zi * ck - zr * sk
        return carry

    lax.fori_loop(0, inner // 8, body, 0)


def outer_inverse(z_ref, xf_ref, c_ref, s_ref, outer):
    inner = c_ref.shape[0]

    def body(i, carry):
        r = pl.multiple_of(i * 8, 8)
        c, s = c_ref[pl.ds(r, 8), :], s_ref[pl.ds(r, 8), :]
        values = []
        for k in range(outer):
            zr = z_ref[k, pl.ds(r, 8), :]
            zi = z_ref[k, pl.ds(pl.multiple_of(inner + r, 8), 8), :]
            ck, sk = c[:, k : k + 1], s[:, k : k + 1]
            values.append((zr * ck - zi * sk, zi * ck + zr * sk))
        values = fft(values, 1)
        for a in range(outer):
            w = math.pi * a / (2 * outer)
            scale = 1.0 / (outer * inner)
            y = values[a][0] * (scale * math.cos(w)) - values[a][1] * (scale * math.sin(w))
            xf_ref[pl.ds(pl.multiple_of(a * inner + r, 8), 8), :] = y
        return carry

    lax.fori_loop(0, inner // 8, body, 0)


def kernel_spectrum_kernel(outer, ker_ref, gh_ref, gl_ref, c_ref, s_ref, out_ref, xf_ref, z_ref):
    inner = c_ref.shape[0]
    for a in range(outer):
        xf_ref[a * inner : (a + 1) * inner, :] = ker_ref[:, a * inner : (a + 1) * inner].T
    outer_forward(xf_ref, z_ref, c_ref, s_ref, outer)

    def body(j, carry):
        z = jnp.concatenate([z_ref[2 * j], z_ref[2 * j + 1]], axis=1)
        h = dot3(gh_ref, gl_ref, z)
        number = h.shape[1] // 2
        out_ref[2 * j] = h[:, :number]
        out_ref[2 * j + 1] = h[:, number:]
        return carry

    lax.fori_loop(0, outer // 2, body, 0)


def conv_kernel_body(outer, *refs):
    sig_ref, spec_ref, gh_ref, gl_ref, ih_ref, il_ref, c_ref, s_ref = refs[:8]
    out_ref, xf_ref, z_ref = refs[-3:]
    inner = c_ref.shape[0]
    xf_ref[...] = sig_ref[...].astype(F32)
    outer_forward(xf_ref, z_ref, c_ref, s_ref, outer)

    def body(j, carry):
        z = jnp.concatenate([z_ref[2 * j], z_ref[2 * j + 1]], axis=1)
        h = jnp.concatenate([spec_ref[2 * j], spec_ref[2 * j + 1]], axis=1)
        f = dot3(gh_ref, gl_ref, z)
        fr, fi = f[:inner], f[inner:]
        hr, hi = h[:inner], h[inner:]
        p = jnp.concatenate([fr * hr - fi * hi, fr * hi + fi * hr], axis=0)
        w = dot3(ih_ref, il_ref, p)
        number = w.shape[1] // 2
        z_ref[2 * j] = w[:, :number]
        z_ref[2 * j + 1] = w[:, number:]
        return carry

    lax.fori_loop(0, outer // 2, body, 0)
    outer_inverse(z_ref, xf_ref, c_ref, s_ref, outer)
    out_ref[...] = xf_ref[...].astype(BF16)


def kernel_spectrum(kernel):
    number, length = kernel.shape
    outer = plan(length)
    inner = length // outer
    (gh, gl), _, c, s = tables(length)
    return pl.pallas_call(
        functools.partial(kernel_spectrum_kernel, outer),
        in_specs=[VMEM] * 5,
        out_specs=VMEM,
        out_shape=jax.ShapeDtypeStruct((outer, 2 * inner, number), F32),
        scratch_shapes=[
            pltpu.VMEM((length, number), F32),
            pltpu.VMEM((outer, 2 * inner, number), F32),
        ],
        compiler_params=params(60),
        cost_estimate=pl.CostEstimate(flops=6 * 10**9, bytes_accessed=7 * 2**20, transcendentals=0),
        name="kernel_spectrum",
    )(kernel, gh, gl, c, s)


def long_conv(signal, spectrum, after):
    length, number = signal.shape
    outer = plan(length)
    inner = length // outer
    (gh, gl), (ih, il), c, s = tables(length)
    return pl.pallas_call(
        functools.partial(conv_kernel_body, outer),
        in_specs=[VMEM] * 8 + [pl.BlockSpec(memory_space=pl.ANY)] * len(after),
        out_specs=VMEM,
        out_shape=jax.ShapeDtypeStruct((length, number), BF16),
        scratch_shapes=[
            pltpu.VMEM((length, number), F32),
            pltpu.VMEM((outer, 2 * inner, number), F32),
        ],
        compiler_params=params(60),
        cost_estimate=pl.CostEstimate(flops=12 * 10**9, bytes_accessed=7 * 2**20, transcendentals=0),
        name="long_conv",
    )(signal, spectrum, gh, gl, ih, il, c, s, *after)


def row_sums(square):
    ones = jnp.ones((8, square.shape[1]), F32)
    return lax.dot_general(
        ones, square, (((1,), (1,)), ((), ())), precision=lax.Precision.HIGHEST, preferred_element_type=F32
    )


def attention_kernel(*refs):
    query_ref = refs[0]
    keys = refs[1 : 2 + SPAN]
    values = refs[2 + SPAN : 3 + 2 * SPAN]
    out_ref, sum_ref, acc_ref = refs[3 + 2 * SPAN :]
    count, width = query_ref.shape
    step = pl.program_id(0)
    me = lax.axis_index("seq")
    odd = lax.rem(me, 2)
    back = [0, 2, 1 + 2 * odd, 3 - 2 * odd]

    @pl.when(step == 0)
    def _():
        acc_ref[...] = jnp.zeros_like(acc_ref)

    row = lax.broadcasted_iota(jnp.int32, (count, count), 0)
    col = lax.broadcasted_iota(jnp.int32, (count, count), 1)
    causal = col <= row
    scale = math.log2(math.e) / math.sqrt(HD)
    for h in range(width // HD):
        lanes = slice(h * HD, (h + 1) * HD)
        q = query_ref[:, lanes]
        scores = []
        for j in range(SPAN + 1):
            s = lax.dot_general(q, keys[j][:, lanes], (((1,), (1,)), ((), ())), preferred_element_type=F32)
            if j == 0:
                s = jnp.where(causal, s, -1e30)
            else:
                s = jnp.where(me >= back[j], s, -1e30)
            scores.append(s)
        peak = functools.reduce(jnp.maximum, scores)
        top = jnp.max(peak, axis=1, keepdims=True)
        numer = jnp.zeros((count, HD), F32)
        total = jnp.zeros((count, count), F32)
        for j in range(SPAN + 1):
            p = jnp.exp2((scores[j] - top) * scale)
            total = total + p
            numer = numer + dot(p.astype(BF16), values[j][:, lanes])
        o = numer / jnp.sum(total, axis=1, keepdims=True)
        out_ref[:, lanes] = o
        acc_ref[...] += o * o

    @pl.when(step == pl.num_programs(0) - 1)
    def _():
        sum_ref[...] = row_sums(acc_ref[...])


def attention(query, keys, values):
    count, width = query.shape
    step = min(width, 256)
    block = pl.BlockSpec((count, step), lambda g: (0, g))
    return pl.pallas_call(
        attention_kernel,
        grid=(width // step,),
        in_specs=[block] * (3 + 2 * SPAN),
        out_specs=[block, pl.BlockSpec((8, count), lambda g: (0, 0))],
        out_shape=[
            jax.ShapeDtypeStruct((count, width), F32),
            jax.ShapeDtypeStruct((8, count), F32),
        ],
        scratch_shapes=[pltpu.VMEM((count, HD), F32)],
        compiler_params=params(60),
        cost_estimate=pl.CostEstimate(flops=5 * 10**9, bytes_accessed=11 * 2**20, transcendentals=4 * 10**6),
        name="attention",
    )(query, *keys, *values)


def mixer_sums_kernel(query_ref, filtered_ref, sum_ref):
    groups, count, lanes = filtered_ref.shape
    acc = jnp.zeros((count, lanes), F32)
    for g in range(groups):
        m = query_ref[:, g * lanes : (g + 1) * lanes].astype(F32) * filtered_ref[g].astype(F32)
        acc = acc + m * m
    sum_ref[...] = row_sums(acc)


def mixer_sums(query, filtered):
    return pl.pallas_call(
        mixer_sums_kernel,
        in_specs=[VMEM] * 2,
        out_specs=VMEM,
        out_shape=jax.ShapeDtypeStruct((8, query.shape[0]), F32),
        compiler_params=params(60),
        name="mixer_sums",
    )(query, filtered)


def join_kernel(attn_ref, query_ref, filtered_ref, asum_ref, msum_ref, beta_a_ref, beta_m_ref, out_ref):
    lanes = filtered_ref.shape[2]
    a_scale = (0.5 * lax.rsqrt(asum_ref[...] / D + EPS)).T[:, 0:1]
    m_scale = (0.5 * lax.rsqrt(msum_ref[...] / D + EPS)).T[:, 0:1]
    for g in range(filtered_ref.shape[0]):
        at = slice(g * lanes, (g + 1) * lanes)
        m = query_ref[:, at].astype(F32) * filtered_ref[g].astype(F32)
        y = beta_a_ref[:, at] * (attn_ref[:, at] * a_scale) + beta_m_ref[:, at] * (m * m_scale)
        out_ref[:, at] = y.astype(BF16)


def join(attn, query, filtered, asum, msum, beta_a, beta_m):
    count, width = query.shape
    step = min(width, 512)
    block = pl.BlockSpec((count, step), lambda g: (0, g))
    sums = pl.BlockSpec((8, count), lambda g: (0, 0))
    beta = pl.BlockSpec((1, step), lambda g: (0, g))
    return pl.pallas_call(
        join_kernel,
        grid=(width // step,),
        in_specs=[block, block, pl.BlockSpec((step // 128, count, 128), lambda g: (g, 0, 0)), sums, sums, beta, beta],
        out_specs=block,
        out_shape=jax.ShapeDtypeStruct((count, width), BF16),
        compiler_params=params(60),
        name="join",
    )(attn, query, filtered, asum, msum, beta_a[None, :], beta_m[None, :])


def on_device(
    mixer_query,
    mixer_key,
    mixer_value,
    shift_taps,
    conv_kernel,
    heads_query,
    heads_key,
    heads_value,
    beta_attention,
    beta_mixer,
):
    count, width = mixer_key.shape
    devices = lax.axis_size("seq")
    number, length = conv_kernel.shape
    before = moved(mixer_key[count - EDGE :], 1)
    before, heads_key, heads_value = lax.optimization_barrier((before, heads_key, heads_value))
    ssm_input = shift_filter(mixer_key, before, mixer_value, shift_taps)
    if number != 128:
        ssm_input = jnp.transpose(ssm_input, (1, 0, 2)).reshape(count, devices, number)
        ssm_input = jnp.transpose(ssm_input, (1, 0, 2))
    signal = lax.all_to_all(ssm_input, "seq", split_axis=0, concat_axis=0, tiled=True)
    spectrum = kernel_spectrum(conv_kernel)
    keys = earlier(heads_key)
    values = earlier(heads_value)
    filtered = long_conv(signal.reshape(length, number), spectrum, keys)
    filtered, *values = lax.optimization_barrier((filtered, *values))
    filtered = filtered.reshape(devices, count, number)
    returned = lax.all_to_all(filtered, "seq", split_axis=0, concat_axis=0, tiled=True)
    if number != 128:
        returned = jnp.transpose(returned, (1, 0, 2)).reshape(count, width // 128, 128)
        returned = jnp.transpose(returned, (1, 0, 2))
    attn, asum = attention(heads_query, [heads_key] + keys, [heads_value] + values)
    msum = mixer_sums(mixer_query, returned)
    asum = lax.psum(asum, "head")
    msum = lax.psum(msum, "head")
    return join(attn, mixer_query, returned, asum, msum, beta_attention, beta_mixer)


def solution(mesh):
    return jax.shard_map(
        on_device,
        mesh=mesh,
        in_specs=(
            P("seq", "head"),
            P("seq", "head"),
            P("seq", "head"),
            P(None, "head"),
            P(("head", "seq"), None),
            P("seq", "head"),
            P("seq", "head"),
            P("seq", "head"),
            P("head"),
            P("head"),
        ),
        out_specs=P("seq", "head"),
        check_vma=False,
    )
```

```python
import functools
import math

import jax
import jax.numpy as jnp
import ml_dtypes
import numpy as np
from jax import lax
from jax.experimental import pallas as pl
from jax.experimental.pallas import tpu as pltpu
from jax.sharding import PartitionSpec as P

D = 4096
HD = 128
TAPS = 8
SPAN = 3
EDGE = 16
EPS = 1e-05
F32 = jnp.float32
BF16 = jnp.bfloat16
VMEM = pl.BlockSpec(memory_space=pltpu.VMEM)


def params(mib, **more):
    return pltpu.CompilerParams(vmem_limit_bytes=mib * 2**20, **more)


def moved(block, distance):
    count = lax.axis_size("seq")
    return lax.ppermute(block, "seq", [(i, i + distance) for i in range(count - distance)])


def routed(block, pairs):
    count = lax.axis_size("seq")
    return lax.ppermute(block, "seq", [(i, j) for i, j in pairs if 0 <= j < count])


def two_back(block):
    return routed(block, [(i, i + 2) for i in range(lax.axis_size("seq"))])


def cross_back(block):
    return routed(block, [(i, i + 1 + 2 * (i % 2)) for i in range(lax.axis_size("seq"))])


def swapped(block):
    return routed(block, [(i, i + 1 - 2 * (i % 2)) for i in range(lax.axis_size("seq"))])


def head_sum(part):
    if lax.axis_size("head") != 2:
        return lax.psum(part, "head")
    return part + lax.ppermute(part, "head", [(0, 1), (1, 0)])


def shift_kernel(key_ref, before_ref, value_ref, taps_ref, out_ref, ext_ref):
    count, width = key_ref.shape
    ext_ref[0:EDGE, :] = before_ref[...].astype(F32)
    ext_ref[EDGE:, :] = key_ref[...].astype(F32)
    total = taps_ref[0:1, :] * ext_ref[EDGE : EDGE + count, :]
    for j in range(1, TAPS):
        total = total + taps_ref[j : j + 1, :] * ext_ref[EDGE - j : EDGE - j + count, :]
    product = (total * value_ref[...].astype(F32)).astype(BF16)
    for g in range(width // 128):
        out_ref[g] = product[:, g * 128 : (g + 1) * 128]


def shift_filter(key, before, value, taps):
    count, width = key.shape
    step = min(width, 512)
    return pl.pallas_call(
        shift_kernel,
        grid=(width // step,),
        in_specs=[
            pl.BlockSpec((count, step), lambda g: (0, g)),
            pl.BlockSpec((EDGE, step), lambda g: (0, g)),
            pl.BlockSpec((count, step), lambda g: (0, g)),
            pl.BlockSpec((TAPS, step), lambda g: (0, g)),
        ],
        out_specs=pl.BlockSpec((step // 128, count, 128), lambda g: (g, 0, 0)),
        out_shape=jax.ShapeDtypeStruct((width // 128, count, 128), BF16),
        scratch_shapes=[pltpu.VMEM((count + EDGE, step), F32)],
        compiler_params=params(60),
        name="shift",
    )(key, before, value, taps)


def fft(values, sign):
    n = len(values)
    if n == 1:
        return values
    even = fft(values[0::2], sign)
    odd = fft(values[1::2], sign)
    low, high = [], []
    for k in range(n // 2):
        er, ei = even[k]
        orr, oi = odd[k]
        if k == 0:
            tr, ti = orr, oi
        elif 4 * k == n:
            tr, ti = (-oi, orr) if sign > 0 else (oi, -orr)
        else:
            c = math.cos(2 * math.pi * k / n)
            s = sign * math.sin(2 * math.pi * k / n)
            if 8 * k == n:
                tr, ti = ((orr - oi) * c, (orr + oi) * c) if sign > 0 else ((orr + oi) * c, (oi - orr) * c)
            elif 8 * k == 3 * n:
                h = -c
                tr, ti = ((-orr - oi) * h, (orr - oi) * h) if sign > 0 else ((oi - orr) * h, (-orr - oi) * h)
            else:
                tr, ti = orr * c - oi * s, orr * s + oi * c
        low.append((er + tr, ei + ti))
        high.append((er - tr, ei - ti))
    return low + high


def plan(length):
    return 32 if length <= 8192 else 64


def split(table):
    high = table.astype(ml_dtypes.bfloat16)
    low = (table - high.astype(np.float64)).astype(ml_dtypes.bfloat16)
    return high, low


def tables(length):
    outer = plan(length)
    inner = length // outer
    period = 2 * length
    b = np.arange(inner)
    angle = 2 * np.pi / inner * (np.outer(b, b) % inner)
    c, s = np.cos(angle), np.sin(angle)
    forward = np.block([[c, s], [-s, c]])
    twist = 2 * np.pi / period * np.outer(b, 2 * np.arange(outer) + 0.5)
    return (
        split(forward),
        split(forward.T),
        np.cos(twist).astype(np.float32),
        np.sin(twist).astype(np.float32),
    )


def dot(a, b):
    return jnp.dot(a, b, preferred_element_type=F32)


def dot3(gh_ref, gl_ref, z):
    zh = z.astype(BF16)
    zl = (z - zh.astype(F32)).astype(BF16)
    gh = gh_ref[...]
    return dot(gh, zh) + dot(gh, zl) + dot(gl_ref[...], zh)


def outer_forward(xf_ref, z_ref, c_ref, s_ref, outer):
    inner = c_ref.shape[0]

    def body(i, carry):
        r = pl.multiple_of(i * 8, 8)
        values = []
        for a in range(outer):
            x = xf_ref[pl.ds(pl.multiple_of(a * inner + r, 8), 8), :]
            w = math.pi * a / (2 * outer)
            values.append((x * math.cos(w), x * (-math.sin(w))))
        values = fft(values, -1)
        c, s = c_ref[pl.ds(r, 8), :], s_ref[pl.ds(r, 8), :]
        for k in range(outer):
            zr, zi = values[k]
            ck, sk = c[:, k : k + 1], s[:, k : k + 1]
            z_ref[k, pl.ds(r, 8), :] = zr * ck + zi * sk
            z_ref[k, pl.ds(pl.multiple_of(inner + r, 8), 8), :] = zi * ck - zr * sk
        return carry

    lax.fori_loop(0, inner // 8, body, 0)


def outer_inverse(z_ref, xf_ref, c_ref, s_ref, outer):
    inner = c_ref.shape[0]

    def body(i, carry):
        r = pl.multiple_of(i * 8, 8)
        c, s = c_ref[pl.ds(r, 8), :], s_ref[pl.ds(r, 8), :]
        values = []
        for k in range(outer):
            zr = z_ref[k, pl.ds(r, 8), :]
            zi = z_ref[k, pl.ds(pl.multiple_of(inner + r, 8), 8), :]
            ck, sk = c[:, k : k + 1], s[:, k : k + 1]
            values.append((zr * ck - zi * sk, zi * ck + zr * sk))
        values = fft(values, 1)
        for a in range(outer):
            w = math.pi * a / (2 * outer)
            scale = 1.0 / (outer * inner)
            y = values[a][0] * (scale * math.cos(w)) - values[a][1] * (scale * math.sin(w))
            xf_ref[pl.ds(pl.multiple_of(a * inner + r, 8), 8), :] = y
        return carry

    lax.fori_loop(0, inner // 8, body, 0)


def kernel_spectrum_kernel(outer, ker_ref, gh_ref, gl_ref, c_ref, s_ref, out_ref, xf_ref, z_ref):
    inner = c_ref.shape[0]
    for a in range(outer):
        xf_ref[a * inner : (a + 1) * inner, :] = ker_ref[:, a * inner : (a + 1) * inner].T
    outer_forward(xf_ref, z_ref, c_ref, s_ref, outer)

    def body(j, carry):
        z = jnp.concatenate([z_ref[2 * j], z_ref[2 * j + 1]], axis=1)
        h = dot3(gh_ref, gl_ref, z)
        number = h.shape[1] // 2
        out_ref[2 * j] = h[:, :number]
        out_ref[2 * j + 1] = h[:, number:]
        return carry

    lax.fori_loop(0, outer // 2, body, 0)


def conv_kernel_body(outer, *refs):
    sig_ref, spec_ref, gh_ref, gl_ref, ih_ref, il_ref, c_ref, s_ref = refs[:8]
    out_ref, xf_ref, z_ref = refs[-3:]
    inner = c_ref.shape[0]
    xf_ref[...] = sig_ref[...].astype(F32)
    outer_forward(xf_ref, z_ref, c_ref, s_ref, outer)

    def body(j, carry):
        z = jnp.concatenate([z_ref[2 * j], z_ref[2 * j + 1]], axis=1)
        h = jnp.concatenate([spec_ref[2 * j], spec_ref[2 * j + 1]], axis=1)
        f = dot3(gh_ref, gl_ref, z)
        fr, fi = f[:inner], f[inner:]
        hr, hi = h[:inner], h[inner:]
        p = jnp.concatenate([fr * hr - fi * hi, fr * hi + fi * hr], axis=0)
        w = dot3(ih_ref, il_ref, p)
        number = w.shape[1] // 2
        z_ref[2 * j] = w[:, :number]
        z_ref[2 * j + 1] = w[:, number:]
        return carry

    lax.fori_loop(0, outer // 2, body, 0)
    outer_inverse(z_ref, xf_ref, c_ref, s_ref, outer)
    out_ref[...] = xf_ref[...].astype(BF16)


def kernel_spectrum(kernel):
    number, length = kernel.shape
    outer = plan(length)
    inner = length // outer
    (gh, gl), _, c, s = tables(length)
    return pl.pallas_call(
        functools.partial(kernel_spectrum_kernel, outer),
        in_specs=[VMEM] * 5,
        out_specs=VMEM,
        out_shape=jax.ShapeDtypeStruct((outer, 2 * inner, number), F32),
        scratch_shapes=[
            pltpu.VMEM((length, number), F32),
            pltpu.VMEM((outer, 2 * inner, number), F32),
        ],
        compiler_params=params(60),
        cost_estimate=pl.CostEstimate(flops=6 * 10**9, bytes_accessed=7 * 2**20, transcendentals=0),
        name="kernel_spectrum",
    )(kernel, gh, gl, c, s)


def long_conv(signal, spectrum, after):
    length, number = signal.shape
    outer = plan(length)
    inner = length // outer
    (gh, gl), (ih, il), c, s = tables(length)
    return pl.pallas_call(
        functools.partial(conv_kernel_body, outer),
        in_specs=[VMEM] * 8 + [pl.BlockSpec(memory_space=pl.ANY)] * len(after),
        out_specs=VMEM,
        out_shape=jax.ShapeDtypeStruct((length, number), BF16),
        scratch_shapes=[
            pltpu.VMEM((length, number), F32),
            pltpu.VMEM((outer, 2 * inner, number), F32),
        ],
        compiler_params=params(60),
        cost_estimate=pl.CostEstimate(flops=12 * 10**9, bytes_accessed=7 * 2**20, transcendentals=0),
        name="long_conv",
    )(signal, spectrum, gh, gl, ih, il, c, s, *after)


def row_sums(square):
    ones = jnp.ones((8, square.shape[1]), F32)
    return lax.dot_general(
        ones, square, (((1,), (1,)), ((), ())), precision=lax.Precision.HIGHEST, preferred_element_type=F32
    )


def attention_kernel(*refs):
    query_ref = refs[0]
    keys = refs[1 : 2 + SPAN]
    values = refs[2 + SPAN : 3 + 2 * SPAN]
    out_ref, sum_ref, acc_ref = refs[3 + 2 * SPAN :]
    count, width = query_ref.shape
    step = pl.program_id(0)
    me = lax.axis_index("seq")
    odd = lax.rem(me, 2)
    back = [0, 2, 1 + 2 * odd, 3 - 2 * odd]

    @pl.when(step == 0)
    def _():
        acc_ref[...] = jnp.zeros_like(acc_ref)

    row = lax.broadcasted_iota(jnp.int32, (count, count), 0)
    col = lax.broadcasted_iota(jnp.int32, (count, count), 1)
    causal = col <= row
    scale = math.log2(math.e) / math.sqrt(HD)
    for h in range(width // HD):
        lanes = slice(h * HD, (h + 1) * HD)
        q = query_ref[:, lanes]
        scores = []
        for j in range(SPAN + 1):
            s = lax.dot_general(q, keys[j][:, lanes], (((1,), (1,)), ((), ())), preferred_element_type=F32)
            if j == 0:
                s = jnp.where(causal, s, -1e30)
            else:
                s = jnp.where(me >= back[j], s, -1e30)
            scores.append(s)
        peak = functools.reduce(jnp.maximum, scores)
        top = jnp.max(peak, axis=1, keepdims=True)
        numer = jnp.zeros((count, HD), F32)
        total = jnp.zeros((count, count), F32)
        for j in range(SPAN + 1):
            p = jnp.exp2((scores[j] - top) * scale)
            total = total + p
            numer = numer + dot(p.astype(BF16), values[j][:, lanes])
        o = numer / jnp.sum(total, axis=1, keepdims=True)
        out_ref[:, lanes] = o
        acc_ref[...] += o * o

    @pl.when(step == pl.num_programs(0) - 1)
    def _():
        sum_ref[...] = row_sums(acc_ref[...])


def attention(query, keys, values):
    count, width = query.shape
    step = min(width, 256)
    block = pl.BlockSpec((count, step), lambda g: (0, g))
    return pl.pallas_call(
        attention_kernel,
        grid=(width // step,),
        in_specs=[block] * (3 + 2 * SPAN),
        out_specs=[block, pl.BlockSpec((8, count), lambda g: (0, 0))],
        out_shape=[
            jax.ShapeDtypeStruct((count, width), F32),
            jax.ShapeDtypeStruct((8, count), F32),
        ],
        scratch_shapes=[pltpu.VMEM((count, HD), F32)],
        compiler_params=params(60),
        cost_estimate=pl.CostEstimate(flops=5 * 10**9, bytes_accessed=11 * 2**20, transcendentals=4 * 10**6),
        name="attention",
    )(query, *keys, *values)


def mixer_sums_kernel(query_ref, filtered_ref, sum_ref):
    groups, count, lanes = filtered_ref.shape
    acc = jnp.zeros((count, lanes), F32)
    for g in range(groups):
        m = query_ref[:, g * lanes : (g + 1) * lanes].astype(F32) * filtered_ref[g].astype(F32)
        acc = acc + m * m
    sum_ref[...] = row_sums(acc)


def mixer_sums(query, filtered):
    return pl.pallas_call(
        mixer_sums_kernel,
        in_specs=[VMEM] * 2,
        out_specs=VMEM,
        out_shape=jax.ShapeDtypeStruct((8, query.shape[0]), F32),
        compiler_params=params(60),
        name="mixer_sums",
    )(query, filtered)


def join_kernel(attn_ref, query_ref, filtered_ref, asum_ref, msum_ref, beta_a_ref, beta_m_ref, out_ref):
    lanes = filtered_ref.shape[2]
    a_scale = (0.5 * lax.rsqrt(asum_ref[...] / D + EPS)).T[:, 0:1]
    m_scale = (0.5 * lax.rsqrt(msum_ref[...] / D + EPS)).T[:, 0:1]
    for g in range(filtered_ref.shape[0]):
        at = slice(g * lanes, (g + 1) * lanes)
        m = query_ref[:, at].astype(F32) * filtered_ref[g].astype(F32)
        y = beta_a_ref[:, at] * (attn_ref[:, at] * a_scale) + beta_m_ref[:, at] * (m * m_scale)
        out_ref[:, at] = y.astype(BF16)


def join(attn, query, filtered, asum, msum, beta_a, beta_m):
    count, width = query.shape
    step = min(width, 512)
    block = pl.BlockSpec((count, step), lambda g: (0, g))
    sums = pl.BlockSpec((8, count), lambda g: (0, 0))
    beta = pl.BlockSpec((1, step), lambda g: (0, g))
    return pl.pallas_call(
        join_kernel,
        grid=(width // step,),
        in_specs=[block, block, pl.BlockSpec((step // 128, count, 128), lambda g: (g, 0, 0)), sums, sums, beta, beta],
        out_specs=block,
        out_shape=jax.ShapeDtypeStruct((count, width), BF16),
        compiler_params=params(60),
        name="join",
    )(attn, query, filtered, asum, msum, beta_a[None, :], beta_m[None, :])


def on_device(
    mixer_query,
    mixer_key,
    mixer_value,
    shift_taps,
    conv_kernel,
    heads_query,
    heads_key,
    heads_value,
    beta_attention,
    beta_mixer,
):
    count, width = mixer_key.shape
    devices = lax.axis_size("seq")
    number, length = conv_kernel.shape
    before = moved(mixer_key[count - EDGE :], 1)
    before, heads_key, heads_value = lax.optimization_barrier((before, heads_key, heads_value))
    ssm_input = shift_filter(mixer_key, before, mixer_value, shift_taps)
    if number != 128:
        ssm_input = jnp.transpose(ssm_input, (1, 0, 2)).reshape(count, devices, number)
        ssm_input = jnp.transpose(ssm_input, (1, 0, 2))
    signal = lax.all_to_all(ssm_input, "seq", split_axis=0, concat_axis=0, tiled=True)
    spectrum = kernel_spectrum(conv_kernel)
    key_two = two_back(heads_key)
    value_two = two_back(heads_value)
    key_cross = cross_back(heads_key)
    value_cross = cross_back(heads_value)
    filtered = long_conv(signal.reshape(length, number), spectrum, [key_two])
    filtered, key_two, key_cross, value_two, value_cross = lax.optimization_barrier(
        (filtered, key_two, key_cross, value_two, value_cross)
    )
    keys = [heads_key, key_two, swapped(key_two), key_cross]
    values = [heads_value, value_two, swapped(value_two), value_cross]
    filtered = filtered.reshape(devices, count, number)
    returned = lax.all_to_all(filtered, "seq", split_axis=0, concat_axis=0, tiled=True)
    if number != 128:
        returned = jnp.transpose(returned, (1, 0, 2)).reshape(count, width // 128, 128)
        returned = jnp.transpose(returned, (1, 0, 2))
    attn, asum = attention(heads_query, keys, values)
    msum = mixer_sums(mixer_query, returned)
    asum = head_sum(asum)
    msum = head_sum(msum)
    return join(attn, mixer_query, returned, asum, msum, beta_attention, beta_mixer)


def solution(mesh):
    return jax.shard_map(
        on_device,
        mesh=mesh,
        in_specs=(
            P("seq", "head"),
            P("seq", "head"),
            P("seq", "head"),
            P(None, "head"),
            P(("head", "seq"), None),
            P("seq", "head"),
            P("seq", "head"),
            P("seq", "head"),
            P("head"),
            P("head"),
        ),
        out_specs=P("seq", "head"),
        check_vma=False,
    )
```
